32 devices in a mesh: section: 2 (over y), expert: 16 (over z, x, core).
Axes of the slice: x: 2, y: 2, z: 4, core: 2. Of those that a mesh axis runs over, the one named last changes fastest.
Arguments:
- section_input: bfloat16 [2, 1536, 2048], P('section', 'expert'), may hold values from -6 to 6
- saved_input: bfloat16 [2, 1536, 2048], P('section', 'expert'), may hold values from -6 to 6
- grad_input: bfloat16 [2, 1536, 2048], P('section', 'expert'), may hold values from -6 to 6
- expert_ids: int32 [2, 2, 1536, 2], P('section', None, 'expert'), may hold values from 0 to 3, all different within a row; in each aligned block of 96 rows (0 to 95, 96 to 191, ..., all dimensions but the last counted through in order) at most 64 rows name the same one
- keep_mask: int32 [2, 2, 1536, 2], P('section', None, 'expert'), may hold values 0 or 1
- norm_gain: float32 [2, 2048], P('section'), may hold values from 0.5 to 1.5
- router_weight: bfloat16 [2, 2048, 4], P('section'), may hold values from -0.25 to 0.25
- gate_weight: bfloat16 [2, 2048, 3072], P('section', None, 'expert'), may hold values from -0.125 to 0.125
- up_weight: bfloat16 [2, 2048, 3072], P('section', None, 'expert'), may hold values from -0.125 to 0.125
- down_weight: bfloat16 [2, 3072, 2048], P('section', 'expert'), may hold values from -0.21875 to 0.21875
Outputs:
- section_output: bfloat16 [2, 1536, 2048], P('section', 'expert')
- grad_output: bfloat16 [2, 1536, 2048], P('section', 'expert')
The draws below stay inside these ranges and needn't reach their ends.
Inputs may be any that keep to these rules, and one draw needn't show every extreme that they name: `expert_ids`: each token names 2 different experts. Among the 96 tokens that one index of expert holds for one section and micro-batch, no expert is named more than 64 times, a bound that some block reaches in some of them.
All inputs are finite; a program needn't handle non-finite values. No bound on the sum of `keep_mask` on one device may be relied on, other than what follows from the above.
Results may differ from the reference program's by a relative error of at most 0.012.
Values may be sent and summed in bfloat16 or wider, within the bound.
A program may use at most 64 MiB of HBM per device.

```python
import math
import jax
import jax.numpy as jnp
import numpy as np
from jax import lax

D = 2048
H = 768
TOP = 2
TOK_MB = 96
SECTIONS = 2
EXPERTS = 4
TOKENS = 1536
MOST = 64
N_SECTION = 2
N_EXPERT = 16


def plant(values, own_key, low, top_value):
    spot = [jax.random.randint(jax.random.fold_in(own_key, axis), (), 0, length) for axis, length in enumerate(values.shape)]
    widest = values.shape.index(max(values.shape))
    neighbour = spot[:widest] + [(spot[widest] + 1) % values.shape[widest]] + spot[widest + 1:]
    return values.at[tuple(spot)].set(low).at[tuple(neighbour)].set(top_value)


def block_scale(stream_key, dims, cuts, smallest, top_value):
    factor_of = 1.0
    for axis_at, blocks in cuts:
        steps = jax.random.uniform(jax.random.fold_in(jax.random.fold_in(stream_key, 6), axis_at), (blocks,), jnp.float32, smallest / len(cuts), top_value / len(cuts))
        factor_of = factor_of * jnp.repeat(jnp.exp(steps), dims[axis_at] // blocks).reshape((-1,) + (1,) * (len(dims) - 1 - axis_at))
    return factor_of


def shared_out(rng, own, number, rows, count, top, reach, lean):
    order = jax.random.permutation(rng, count)
    heavy_load, usual = shares(count, rows * top, reach, lean, True), shares(count, rows * top, reach, lean, False)
    places = jnp.arange(count)

    def named(sizes, rotation):
        used = int((sizes > 0).sum())
        fixed = max(1, used // 4)
        shifted = fixed + (places - fixed + rotation * (used - fixed)) % max(1, count - fixed)
        return jnp.zeros((count,), jnp.int32).at[order[jnp.where(places < fixed, places, shifted)]].set(jnp.asarray(sizes, jnp.int32))

    sizes = jnp.where(number % 4 == 0, named(heavy_load, number // 4), named(usual, number - number // 4 - 1))
    mixed = jax.random.permutation(jax.random.fold_in(own, 3), count)
    source_of, receiver = mixed[0:count // 2 * 2:2], mixed[1:count // 2 * 2:2]
    margin = jnp.minimum(sizes[source_of] - 1, reach - sizes[receiver]) // 2
    margin = jnp.where((source_of == order[0]) | (receiver == order[0]) | (sizes[receiver] == 0), 0, jnp.maximum(margin, 0))
    shifted = jax.random.randint(jax.random.fold_in(own, 4), (count // 2,), 0, 1 << 20) % (margin + 1)
    sizes = sizes.at[source_of].add(-shifted).at[receiver].add(shifted)
    labels = jnp.searchsorted(jnp.cumsum(sizes), jnp.arange(rows * top), side="right").astype(jnp.int32)
    table = labels.reshape(top, rows).T
    table = table[jax.random.permutation(jax.random.fold_in(own, 1), rows)]
    rotation = jax.random.randint(jax.random.fold_in(own, 2), (rows, 1), 0, top)
    return jnp.take_along_axis(table, (jnp.arange(top)[None, :] + rotation) % top, axis=1)


def shares(number_of, total, bound, lean, full):
    weights = [(1 << 20) // math.isqrt(standing ** lean) + 1 for standing in range(1, number_of + 1)]
    largest = bound if full else min(bound, max(-(-total // number_of), total * weights[0] // sum(weights)))
    least = 1 if total - largest >= number_of - 1 else 0
    given, surplus = [largest] + [least] * (number_of - 1), total - largest - least * (number_of - 1)
    while surplus > 0:
        movable = [i for i in range(1, number_of) if given[i] < largest] or [i for i in range(1, number_of) if given[i] < bound]
        mass, budget = sum([weights[i] for i in movable]), surplus
        for i in movable:
            addition = min(bound - given[i], max(1, budget * weights[i] // mass), surplus)
            given[i] = given[i] + addition
            surplus = surplus - addition
    return np.array(given)


def gaussian(rng, extent, scale, bound, pieces=(), kind=jnp.bfloat16):
    values = jax.random.normal(rng, extent, jnp.float32) * scale
    if len(pieces) > 0:
        values = block_scale(rng, extent, pieces, -0.22, 0.18) * values
    return jnp.clip(values, min=-bound, max=bound).astype(kind)


def setup_inputs(seed: int = 0) -> dict:
    key_list = jax.random.split(jax.random.key(seed), 11)
    section_input = gaussian(key_list[0], (SECTIONS, TOKENS, D), 1.0, 6.0, ((0, 2), (1, 16)))
    saved_input = gaussian(key_list[1], (SECTIONS, TOKENS, D), 1.0, 6.0, ((0, 2), (1, 16)))
    grad_input = gaussian(key_list[2], (SECTIONS, TOKENS, D), 1.0, 6.0, ((0, 2), (1, 16)))
    expert_ids_keys = jax.random.split(jax.random.fold_in(key_list[3], 1), SECTIONS * 2 * TOKENS // TOK_MB)
    expert_ids_turns = jax.random.permutation(jax.random.fold_in(key_list[3], 3), SECTIONS * 2 * TOKENS // TOK_MB)
    expert_ids = jax.vmap(lambda own, number: shared_out(jax.random.fold_in(key_list[3], 2), own, number, TOK_MB, EXPERTS, TOP, MOST, 2))(expert_ids_keys, expert_ids_turns).reshape((SECTIONS, 2, TOKENS, TOP))
    keep_mask = plant((jax.random.randint(key_list[4], (SECTIONS, 2, TOKENS, TOP), 0, 8) < 7).astype(jnp.int32), jax.random.fold_in(key_list[4], 1), 0, 1)
    norm_gain = jnp.clip(0.5 + 1.0 * jax.random.uniform(key_list[5], (SECTIONS, D), jnp.float32) ** block_scale(key_list[5], (SECTIONS, D), ((0, 2),), -0.2, 0.2), 0.5, 1.5)
    router_weight = gaussian(key_list[6], (SECTIONS, D, EXPERTS), (D // 4) ** -0.5, 0.25, ((0, 2),))
    gate_weight = gaussian(key_list[7], (SECTIONS, D, EXPERTS * H), D ** -0.5, 0.125, ((0, 2), (2, 16)))
    up_weight = gaussian(key_list[8], (SECTIONS, D, EXPERTS * H), D ** -0.5, 0.125, ((0, 2), (2, 16)))
    down_weight = gaussian(key_list[9], (SECTIONS, EXPERTS * H, D), H ** -0.5, 0.21875, ((0, 2), (1, 16)))
    return {"section_input": section_input, "saved_input": saved_input, "grad_input": grad_input, "expert_ids": expert_ids, "keep_mask": keep_mask, "norm_gain": norm_gain, "router_weight": router_weight, "gate_weight": gate_weight, "up_weight": up_weight, "down_weight": down_weight}


EPS = 1e-06
KEEP_SCALE = 8.0 / 7.0

def normalize(hidden, gain_row):
    plain = hidden.astype(jnp.float32)
    inverse = lax.rsqrt(lax.optimization_barrier(jnp.mean(plain * plain, axis=-1, keepdims=True)) + EPS)
    return (plain, inverse, (plain * inverse * gain_row).astype(jnp.bfloat16))

def gating(normed, router_layer, chosen_ids, keep_bits):
    logits = jnp.dot(normed, router_layer, preferred_element_type=jnp.float32)
    picked = jnp.take_along_axis(logits, chosen_ids, axis=1)
    spread = jnp.exp(picked[:, None, :] - picked[:, :, None])
    gate_probs = 1.0 / lax.optimization_barrier(jnp.sum(spread, axis=2))
    return (gate_probs, keep_bits.astype(jnp.float32) * KEEP_SCALE * gate_probs)

def expert_forward(row_block, gate_full, up_full, down_full):
    pre_gate = jnp.dot(row_block, gate_full, preferred_element_type=jnp.float32)
    pre_up = jnp.dot(row_block, up_full, preferred_element_type=jnp.float32)
    inner_act = (pre_gate * jax.nn.sigmoid(pre_gate) * pre_up).astype(jnp.bfloat16)
    return jnp.dot(inner_act, down_full, preferred_element_type=jnp.float32).astype(jnp.bfloat16)

def expert_backward(row_block, upstream, gate_full, up_full, down_full):
    pre_gate = jnp.dot(row_block, gate_full, preferred_element_type=jnp.float32)
    pre_up = jnp.dot(row_block, up_full, preferred_element_type=jnp.float32)
    sigma_gate = jax.nn.sigmoid(pre_gate)
    inner_act = (pre_gate * sigma_gate * pre_up).astype(jnp.bfloat16)
    pulled = jnp.dot(upstream, down_full.T, preferred_element_type=jnp.float32)
    gate_change = lax.optimization_barrier(jnp.sum(inner_act.astype(jnp.float32) * pulled, axis=1)).astype(jnp.bfloat16)
    grad_gate = (pulled * pre_up * sigma_gate * (1.0 + pre_gate * (1.0 - sigma_gate))).astype(jnp.bfloat16)
    grad_up = (pulled * pre_gate * sigma_gate).astype(jnp.bfloat16)
    back_sum = jnp.dot(grad_gate, gate_full.T, preferred_element_type=jnp.float32)
    back_sum = back_sum + jnp.dot(grad_up, up_full.T, preferred_element_type=jnp.float32)
    return (back_sum.astype(jnp.bfloat16), gate_change)

def source_backward(plain, inverse, gain_row, router_layer, chosen_ids, keep_bits, gate_probs, scale, upstream, returned, gate_change):
    change = keep_bits.astype(jnp.float32) * KEEP_SCALE * gate_change.astype(jnp.float32)
    logit_grad = gate_probs * (change - lax.optimization_barrier(jnp.sum(gate_probs * change, axis=1, keepdims=True)))
    onehot = (chosen_ids[:, :, None] == jnp.arange(EXPERTS, dtype=jnp.int32)[None, None, :]).astype(jnp.float32)
    dense_grad = lax.optimization_barrier(jnp.sum(logit_grad[:, :, None] * onehot, axis=1))
    through_router = lax.dot_general(dense_grad, router_layer.astype(jnp.float32), (((1,), (1,)), ((), ())), precision=lax.Precision.HIGHEST, preferred_element_type=jnp.float32)
    total_grad = lax.optimization_barrier(jnp.sum(scale[:, :, None] * returned.astype(jnp.float32), axis=1)) + through_router
    weighted = total_grad * gain_row
    inner_mean = lax.optimization_barrier(jnp.mean(weighted * plain, axis=-1, keepdims=True))
    norm_grad = inverse * (weighted - plain * inverse * inverse * inner_mean)
    return (upstream.astype(jnp.float32) + norm_grad).astype(jnp.bfloat16)

def expert_block(gate_layer, up_layer, down_layer, expert):
    first_col = (expert * H).astype(jnp.int32)
    return (lax.dynamic_slice_in_dim(gate_layer, first_col, H, 1), lax.dynamic_slice_in_dim(up_layer, first_col, H, 1), lax.dynamic_slice_in_dim(down_layer, first_col, H, 0))

def by_expert(flat_ids, compute):
    count_all = flat_ids.shape[0]
    max_rows = min(N_EXPERT * MOST, count_all)
    sort_order = jnp.argsort(flat_ids, stable=True).astype(jnp.int32)
    counts = lax.optimization_barrier(jnp.sum((flat_ids[:, None] == jnp.arange(EXPERTS, dtype=jnp.int32)[None, :]).astype(jnp.int32), axis=0)).astype(jnp.int32)
    starts = (jnp.cumsum(counts) - counts).astype(jnp.int32)
    padded = jnp.concatenate([sort_order, jnp.full((max_rows,), count_all, jnp.int32)])

    def single(expert):
        picked_rows = lax.dynamic_slice(padded, (starts[expert],), (max_rows,))
        valid_rows = jnp.arange(max_rows, dtype=jnp.int32) < counts[expert]
        picked_rows = jnp.where(valid_rows, picked_rows, count_all).astype(jnp.int32)
        return (picked_rows, compute(expert, jnp.minimum(picked_rows, count_all - 1).astype(jnp.int32)))
    picked_all, results = lax.map(single, jnp.arange(EXPERTS, dtype=jnp.int32))
    flat_picks = picked_all.reshape(-1)

    def place_rows(values):
        tail_shape = values.shape[2:]
        table_rows = jnp.zeros((count_all + 1,) + tail_shape, values.dtype)
        return table_rows.at[flat_picks].set(values.reshape((-1,) + tail_shape))[:count_all]
    return jax.tree.map(place_rows, results)

def reference(section_input, saved_input, grad_input, expert_ids, keep_mask, norm_gain, router_weight, gate_weight, up_weight, down_weight):
    output_list = []
    grad_list = []
    for section_index in range(N_SECTION):
        gain_row = norm_gain[section_index]
        router_layer = router_weight[section_index]
        gate_layer = gate_weight[section_index]
        up_layer = up_weight[section_index]
        down_layer = down_weight[section_index]
        forward_ids = expert_ids[section_index, 0]
        backward_ids = expert_ids[section_index, 1]
        forward_plain, forward_inverse, forward_normed = normalize(section_input[section_index], gain_row)
        forward_probs, forward_scale = gating(forward_normed, router_layer, forward_ids, keep_mask[section_index, 0])

        def forward_rows(expert, picked_rows):
            gate_full, up_full, down_full = expert_block(gate_layer, up_layer, down_layer, expert)
            return expert_forward(forward_normed[picked_rows // TOP], gate_full, up_full, down_full)
        copies = by_expert(forward_ids.reshape(-1), forward_rows).reshape(TOKENS, TOP, D)
        mixed_out = forward_plain + lax.optimization_barrier(jnp.sum(forward_scale[:, :, None] * copies.astype(jnp.float32), axis=1))
        output_list.append(mixed_out.astype(jnp.bfloat16))
        backward_plain, backward_inverse, backward_normed = normalize(saved_input[section_index], gain_row)
        backward_probs, backward_scale = gating(backward_normed, router_layer, backward_ids, keep_mask[section_index, 1])
        upstream_all = grad_input[section_index]

        def backward_rows(expert, picked_rows):
            gate_full, up_full, down_full = expert_block(gate_layer, up_layer, down_layer, expert)
            owner_token = picked_rows // TOP
            return expert_backward(backward_normed[owner_token], upstream_all[owner_token], gate_full, up_full, down_full)
        returned_flat, change_flat = by_expert(backward_ids.reshape(-1), backward_rows)
        grad_list.append(source_backward(backward_plain, backward_inverse, gain_row, router_layer, backward_ids, keep_mask[section_index, 1], backward_probs, backward_scale, upstream_all, returned_flat.reshape(TOKENS, TOP, D), change_flat.reshape(TOKENS, TOP)))
    section_output = jnp.roll(jnp.stack(output_list), 1, axis=0)
    grad_output = jnp.roll(jnp.stack(grad_list), -1, axis=0)
    return (section_output, grad_output)
```

```python
import functools

import jax
import jax.numpy as jnp
from jax import lax
from jax.experimental import pallas as pl
from jax.experimental.pallas import tpu as pltpu
from jax.sharding import PartitionSpec as P

EPS = 1e-06
KEEP_SCALE = 8.0 / 7.0
MESH = pl.DeviceIdType.MESH
F32 = jnp.float32
BF16 = jnp.bfloat16


def rows_by_rows(left, right):
    return lax.dot_general(left, right, (((1,), (1,)), ((), ())), preferred_element_type=F32)


def matmul(left, right):
    return jnp.dot(left, right, preferred_element_type=F32)


def normalize(hidden, gain):
    plain = hidden.astype(F32)
    inverse = lax.rsqrt(jnp.mean(plain * plain, axis=-1, keepdims=True) + EPS)
    return inverse, (plain * inverse * gain).astype(BF16)


def routing(normed, router, ids, keep, capacity):
    tokens, experts = normed.shape[0], router.shape[1]
    top = ids.shape[1]
    logits = matmul(normed, router)
    lane = lax.broadcasted_iota(jnp.int32, (tokens, experts), 1)
    chosen = [ids[:, k : k + 1] == lane for k in range(top)]
    picked = [jnp.sum(jnp.where(c, logits, 0.0), axis=1, keepdims=True) for c in chosen]
    probs = []
    for k in range(top):
        spread = functools.reduce(jnp.add, [jnp.exp(p - picked[k]) for p in picked])
        probs.append(1.0 / spread)
    kept = [keep[:, k : k + 1].astype(F32) * KEEP_SCALE for k in range(top)]
    scale = [kept[k] * probs[k] for k in range(top)]
    named = functools.reduce(jnp.add, [jnp.where(c, 1.0, 0.0) for c in chosen])
    row = lax.broadcasted_iota(jnp.int32, (tokens, tokens), 0)
    column = lax.broadcasted_iota(jnp.int32, (tokens, tokens), 1)
    earlier = jnp.where(column < row, 1.0, 0.0).astype(BF16)
    rank = matmul(earlier, named.astype(BF16))
    place = lane.astype(F32) * capacity + rank
    slot = [jnp.sum(jnp.where(c, place, 0.0), axis=1, keepdims=True) for c in chosen]
    along = [jnp.sum(jnp.where(row == column, s, 0.0), axis=0, keepdims=True) for s in slot]
    table = lax.broadcasted_iota(jnp.int32, (experts * capacity, tokens), 0).astype(F32)
    fill = functools.reduce(jnp.add, [jnp.where(table == a, 1.0, 0.0) for a in along]).astype(BF16)
    return chosen, probs, kept, scale, slot, fill


def pickers(slot, slots):
    tokens = slot[0].shape[0]
    lane = lax.broadcasted_iota(jnp.int32, (tokens, slots), 1).astype(F32)
    return [jnp.where(lane == s, 1.0, 0.0).astype(BF16) for s in slot]


def layer(
    experts,
    replicas,
    sections,
    capacity,
    fwd_in,
    bwd_in,
    grad_in,
    ids_ref,
    keep_ref,
    gain_ref,
    router_ref,
    gate_ref,
    up_ref,
    down_ref,
    fwd_out,
    bwd_out,
    w_gate,
    w_up,
    w_down,
    sent,
    got,
    done,
    back,
    change_done,
    change_back,
    inner,
    grad_gate,
    grad_up,
    weighted,
    staged,
    quarter_send,
    quarter_recv,
    row_send,
    row_recv,
    back_send,
    back_recv,
    hand_send,
    hand_recv,
):
    section = lax.axis_index("section")
    me = lax.axis_index("expert")
    group, replica = me // replicas, me % replicas
    tokens, width = fwd_in.shape
    quarter = down_ref.shape[0]
    hidden = quarter * replicas
    slots = experts * capacity
    core_mate = group * replicas + (replica + 1 - 2 * (replica % 2))
    chip_mate = group * replicas + (replica + 2) % replicas
    following = (section + 1) % sections
    previous = (section + sections - 1) % sections

    barrier = pltpu.get_barrier_semaphore()
    mates = [{"expert": core_mate}, {"expert": chip_mate}]
    mates += [{"section": following}, {"section": previous}]
    others = [(group + d) % experts for d in range(1, experts)]
    mates += [{"expert": other * replicas + replica} for other in others]
    for mate in mates:
        pl.semaphore_signal(barrier, inc=1, device_id=mate, device_id_type=MESH)
    pl.semaphore_wait(barrier, len(mates))

    weights = [w_down, w_gate, w_up]
    started = []

    def quarter_copy(which, place, mate, source):
        copy = pltpu.make_async_remote_copy(
            src_ref=source,
            dst_ref=weights[which].at[pl.ds(place * quarter, quarter)],
            send_sem=quarter_send.at[place, which],
            recv_sem=quarter_recv.at[place, which],
            device_id={"expert": mate},
            device_id_type=MESH,
        )
        copy.start()
        started.append(copy)
        return copy

    def row_block(ref, index):
        return ref.at[pl.ds(pl.multiple_of(index * capacity, capacity), capacity)]

    def trade(source, target, send_sem, recv_sem):
        copies = []
        for place, other in enumerate(others):
            copy = pltpu.make_async_remote_copy(
                src_ref=row_block(source, other),
                dst_ref=row_block(target, group),
                send_sem=send_sem.at[place],
                recv_sem=recv_sem.at[place],
                device_id={"expert": other * replicas + replica},
                device_id_type=MESH,
            )
            copy.start()
            copies.append(copy)
        started.extend(copies)
        own = pl.ds(pl.multiple_of(group * capacity, capacity), capacity)
        target[own, :] = source[own, :]
        return copies

    across = [quarter_copy(0, 2, chip_mate, down_ref)]
    quarter_copy(0, 1, core_mate, down_ref)

    gain = gain_ref[...]
    router = router_ref[...]
    fwd_inverse, fwd_normed = normalize(fwd_in[...], gain)
    del fwd_inverse
    fwd_route = routing(fwd_normed, router, ids_ref[0], keep_ref[0], capacity)
    sent[0] = matmul(fwd_route[5], fwd_normed).astype(BF16)
    moves = [trade(sent.at[0], got.at[0], row_send.at[0], row_recv.at[0])]

    eye = jnp.where(
        lax.broadcasted_iota(jnp.int32, (quarter, quarter), 0)
        == lax.broadcasted_iota(jnp.int32, (quarter, quarter), 1),
        1.0,
        0.0,
    ).astype(BF16)
    for which, source, target in ((1, gate_ref, w_gate), (2, up_ref, w_up)):
        target[0:quarter, :] = rows_by_rows(eye, source[...]).astype(BF16)
        own_piece = target.at[pl.ds(0, quarter)]
        across.append(quarter_copy(which, 2, chip_mate, own_piece))
        quarter_copy(which, 1, core_mate, own_piece)
    w_down[0:quarter, :] = down_ref[...]

    bwd_inverse, bwd_normed = normalize(bwd_in[...], gain)
    bwd_route = routing(bwd_normed, router, ids_ref[1], keep_ref[1], capacity)
    sent[1] = matmul(bwd_route[5], bwd_normed).astype(BF16)
    moves.append(trade(sent.at[1], got.at[1], row_send.at[1], row_recv.at[1]))
    sent[2] = matmul(bwd_route[5], grad_in[...]).astype(BF16)
    moves.append(trade(sent.at[2], got.at[2], row_send.at[2], row_recv.at[2]))

    for which, copy in enumerate(across):
        copy.wait_recv()
        quarter_copy(which, 3, core_mate, weights[which].at[pl.ds(2 * quarter, quarter)])
    for place in (1, 3):
        for which in range(3):
            pltpu.make_async_remote_copy(
                src_ref=down_ref,
                dst_ref=weights[which].at[pl.ds(place * quarter, quarter)],
                send_sem=quarter_send.at[place, which],
                recv_sem=quarter_recv.at[place, which],
                device_id={"expert": core_mate},
                device_id_type=MESH,
            ).wait_recv()

    step = 256 if hidden % 256 == 0 else quarter
    wide = 512 if width % 512 == 0 else width

    def part(index, size):
        return pl.ds(pl.multiple_of(index * size, size), size)

    for copy in moves[0]:
        copy.wait_recv()

    @pl.loop(0, hidden // step)
    def _(h):
        rows = got[0]
        pre_gate = rows_by_rows(rows, w_gate[part(h, step), :])
        pre_up = rows_by_rows(rows, w_up[part(h, step), :])
        inner[:, part(h, step)] = (pre_gate * jax.nn.sigmoid(pre_gate) * pre_up).astype(BF16)

    @pl.loop(0, width // wide)
    def _(c):
        done[0, :, part(c, wide)] = matmul(inner[...], w_down[:, part(c, wide)]).astype(BF16)

    returns = [trade(done.at[0], back.at[0], back_send.at[0], back_recv.at[0])]

    for copy in moves[1] + moves[2]:
        copy.wait_recv()

    def backward_step(h, change):
        rows = got[1]
        pre_gate = rows_by_rows(rows, w_gate[part(h, step), :])
        pre_up = rows_by_rows(rows, w_up[part(h, step), :])
        pulled = rows_by_rows(got[2], w_down[part(h, step), :])
        sigma = jax.nn.sigmoid(pre_gate)
        act = (pre_gate * sigma * pre_up).astype(BF16).astype(F32)
        grad_gate[:, part(h, step)] = (
            pulled * pre_up * sigma * (1.0 + pre_gate * (1.0 - sigma))
        ).astype(BF16)
        grad_up[:, part(h, step)] = (pulled * pre_gate * sigma).astype(BF16)
        return change + jnp.sum(act * pulled, axis=1, keepdims=True)

    change = lax.fori_loop(0, hidden // step, backward_step, jnp.zeros((slots, 1), F32))
    change_done[...] = jnp.broadcast_to(change, change_done.shape).astype(BF16)
    change_moves = trade(change_done, change_back, back_send.at[2], back_recv.at[2])

    @pl.loop(0, width // wide)
    def _(c):
        total = matmul(grad_gate[...], w_gate[:, part(c, wide)])
        total += matmul(grad_up[...], w_up[:, part(c, wide)])
        done[1, :, part(c, wide)] = total.astype(BF16)

    returns.append(trade(done.at[1], back.at[1], back_send.at[1], back_recv.at[1]))

    for copy in returns[0]:
        copy.wait_recv()
    fwd_pick = pickers(fwd_route[4], slots)
    fwd_scale = fwd_route[3]

    @pl.loop(0, width // wide)
    def _(c):
        total = fwd_in[:, part(c, wide)].astype(F32)
        mixed = None
        for pick, scale in zip(fwd_pick, fwd_scale):
            term = scale * matmul(pick, back[0, :, part(c, wide)])
            mixed = term if mixed is None else mixed + term
        staged[0, :, part(c, wide)] = (total + mixed).astype(BF16)

    hand_fwd = pltpu.make_async_remote_copy(
        src_ref=staged.at[0],
        dst_ref=fwd_out.at[0],
        send_sem=hand_send.at[0],
        recv_sem=hand_recv.at[0],
        device_id={"section": following},
        device_id_type=MESH,
    )
    hand_fwd.start()

    for copy in change_moves + returns[1]:
        copy.wait_recv()
    chosen, probs, kept, scale, slot, _ = bwd_route
    pick = pickers(slot, slots)
    moved = [kept[k] * matmul(pick[k], change_back[...])[:, 0:1] for k in range(len(pick))]
    balance = functools.reduce(jnp.add, [probs[k] * moved[k] for k in range(len(pick))])
    logit_grad = [probs[k] * (moved[k] - balance) for k in range(len(pick))]
    dense = functools.reduce(
        jnp.add, [jnp.where(chosen[k], logit_grad[k], 0.0) for k in range(len(pick))]
    )
    dense_high = dense.astype(BF16)
    dense_low = (dense - dense_high.astype(F32)).astype(BF16)

    def gather_step(c, dots):
        total = None
        for k in range(len(pick)):
            term = scale[k] * matmul(pick[k], back[1, :, part(c, wide)])
            total = term if total is None else total + term
        near_router = router_ref[part(c, wide), :]
        total += rows_by_rows(dense_high, near_router) + rows_by_rows(dense_low, near_router)
        gained = total * gain_ref[:, part(c, wide)]
        weighted[:, part(c, wide)] = gained
        plain = bwd_in[:, part(c, wide)].astype(F32)
        return dots + jnp.sum(gained * plain, axis=1, keepdims=True)

    dots = lax.fori_loop(0, width // wide, gather_step, jnp.zeros((tokens, 1), F32))
    factor = bwd_inverse * bwd_inverse * (dots * (1.0 / width))

    @pl.loop(0, width // wide)
    def _(c):
        plain = bwd_in[:, part(c, wide)].astype(F32)
        norm_grad = bwd_inverse * (weighted[:, part(c, wide)] - plain * factor)
        staged[1, :, part(c, wide)] = (grad_in[:, part(c, wide)].astype(F32) + norm_grad).astype(
            BF16
        )

    hand_bwd = pltpu.make_async_remote_copy(
        src_ref=staged.at[1],
        dst_ref=bwd_out.at[0],
        send_sem=hand_send.at[1],
        recv_sem=hand_recv.at[1],
        device_id={"section": previous},
        device_id_type=MESH,
    )
    hand_bwd.start()
    for copy in started:
        copy.wait_send()
    hand_fwd.wait()
    hand_bwd.wait()


def on_device(
    section_input,
    saved_input,
    grad_input,
    expert_ids,
    keep_mask,
    norm_gain,
    router_weight,
    gate_weight,
    up_weight,
    down_weight,
):
    tokens, width = section_input.shape[1:]
    experts = router_weight.shape[2]
    top = expert_ids.shape[3]
    replicas = lax.axis_size("expert") // experts
    sections = lax.axis_size("section")
    capacity = 4 * tokens * top // (3 * experts)
    slots = experts * capacity
    quarter = down_weight.shape[1]
    hidden = quarter * replicas
    dma = pltpu.SemaphoreType.DMA
    vmem = pl.BlockSpec(memory_space=pltpu.VMEM)
    result = jax.ShapeDtypeStruct((1, tokens, width), BF16)
    return pl.pallas_call(
        functools.partial(layer, experts, replicas, sections, capacity),
        out_shape=(result, result),
        in_specs=[vmem] * 10,
        out_specs=(pl.BlockSpec(memory_space=pl.ANY),) * 2,
        scratch_shapes=[
            pltpu.VMEM((hidden, width), BF16),
            pltpu.VMEM((hidden, width), BF16),
            pltpu.VMEM((hidden, width), BF16),
            pltpu.VMEM((3, slots, width), BF16),
            pltpu.VMEM((3, slots, width), BF16),
            pltpu.VMEM((2, slots, width), BF16),
            pltpu.VMEM((2, slots, width), BF16),
            pltpu.VMEM((slots, 128), BF16),
            pltpu.VMEM((slots, 128), BF16),
            pltpu.VMEM((slots, hidden), BF16),
            pltpu.VMEM((slots, hidden), BF16),
            pltpu.VMEM((slots, hidden), BF16),
            pltpu.VMEM((tokens, width), F32),
            pltpu.VMEM((2, tokens, width), BF16),
            dma((4, 3)),
            dma((4, 3)),
            dma((3, experts - 1)),
            dma((3, experts - 1)),
            dma((3, experts - 1)),
            dma((3, experts - 1)),
            dma((2,)),
            dma((2,)),
        ],
        compiler_params=pltpu.CompilerParams(
            collective_id=0, has_side_effects=True, vmem_limit_bytes=56 * 1024 * 1024
        ),
    )(
        section_input[0],
        saved_input[0],
        grad_input[0],
        expert_ids[0],
        keep_mask[0],
        norm_gain,
        router_weight[0],
        gate_weight[0],
        up_weight[0],
        down_weight[0],
    )


def solution(mesh):
    return jax.shard_map(
        on_device,
        mesh=mesh,
        in_specs=(
            P("section", "expert", None),
            P("section", "expert", None),
            P("section", "expert", None),
            P("section", None, "expert", None),
            P("section", None, "expert", None),
            P("section", None),
            P("section", None, None),
            P("section", None, "expert"),
            P("section", None, "expert"),
            P("section", "expert", None),
        ),
        out_specs=(P("section", "expert", None), P("section", "expert", None)),
        check_vma=False,
    )
```

```python
import functools

import jax
import jax.numpy as jnp
from jax import lax
from jax.experimental import pallas as pl
from jax.experimental.pallas import tpu as pltpu
from jax.sharding import PartitionSpec as P

EPS = 1e-06
KEEP_SCALE = 8.0 / 7.0
MESH = pl.DeviceIdType.MESH
F32 = jnp.float32
BF16 = jnp.bfloat16


def rows_by_rows(left, right):
    return lax.dot_general(left, right, (((1,), (1,)), ((), ())), preferred_element_type=F32)


def matmul(left, right):
    return jnp.dot(left, right, preferred_element_type=F32)


def normalize(hidden, gain):
    plain = hidden.astype(F32)
    inverse = lax.rsqrt(jnp.mean(plain * plain, axis=-1, keepdims=True) + EPS)
    return inverse, (plain * inverse * gain).astype(BF16)


def routing(normed, router, id_rows, keep_rows, capacity):
    tokens, experts = normed.shape[0], router.shape[0]
    top = id_rows.shape[0]
    logits = rows_by_rows(normed, router)
    lane = lax.broadcasted_iota(jnp.int32, (tokens, experts), 1)
    row = lax.broadcasted_iota(jnp.int32, (tokens, tokens), 0)
    column = lax.broadcasted_iota(jnp.int32, (tokens, tokens), 1)

    def upright(line):
        spread_out = jnp.where(row == column, line.astype(F32), 0.0)
        return jnp.sum(spread_out, axis=1, keepdims=True)

    ids = [upright(id_rows[k : k + 1, :]) for k in range(top)]
    chosen = [i == lane.astype(F32) for i in ids]
    picked = [jnp.sum(jnp.where(c, logits, 0.0), axis=1, keepdims=True) for c in chosen]
    probs = []
    for k in range(top):
        spread = functools.reduce(jnp.add, [jnp.exp(p - picked[k]) for p in picked])
        probs.append(1.0 / spread)
    kept = [upright(keep_rows[k : k + 1, :]) * KEEP_SCALE for k in range(top)]
    scale = [kept[k] * probs[k] for k in range(top)]
    named = functools.reduce(jnp.add, [jnp.where(c, 1.0, 0.0) for c in chosen])
    earlier = jnp.where(column < row, 1.0, 0.0).astype(BF16)
    rank = matmul(earlier, named.astype(BF16))
    place = lane.astype(F32) * capacity + rank
    slot = [jnp.sum(jnp.where(c, place, 0.0), axis=1, keepdims=True) for c in chosen]
    along = [jnp.sum(jnp.where(row == column, s, 0.0), axis=0, keepdims=True) for s in slot]
    table = lax.broadcasted_iota(jnp.int32, (experts * capacity, tokens), 0).astype(F32)
    fill = functools.reduce(jnp.add, [jnp.where(table == a, 1.0, 0.0) for a in along]).astype(BF16)
    return chosen, probs, kept, scale, slot, fill


def pickers(slot, slots):
    tokens = slot[0].shape[0]
    lane = lax.broadcasted_iota(jnp.int32, (tokens, slots), 1).astype(F32)
    return [jnp.where(lane == s, 1.0, 0.0).astype(BF16) for s in slot]


def layer(
    experts,
    replicas,
    sections,
    capacity,
    fwd_in,
    bwd_in,
    grad_in,
    ids_ref,
    keep_ref,
    gain_ref,
    router_ref,
    gate_ref,
    up_ref,
    down_ref,
    fwd_out,
    bwd_out,
    w_gate,
    w_up,
    w_down,
    sent,
    got,
    done,
    back,
    change_done,
    change_back,
    inner,
    grad_gate,
    grad_up,
    weighted,
    staged,
    quarter_send,
    quarter_recv,
    row_send,
    row_recv,
    back_send,
    back_recv,
    hand_send,
    hand_recv,
):
    section = lax.axis_index("section")
    me = lax.axis_index("expert")
    group, replica = me // replicas, me % replicas
    tokens, width = fwd_in.shape
    quarter = down_ref.shape[0]
    hidden = quarter * replicas
    slots = experts * capacity
    core_mate = group * replicas + (replica + 1 - 2 * (replica % 2))
    chip_mate = group * replicas + (replica + 2) % replicas
    following = (section + 1) % sections
    previous = (section + sections - 1) % sections

    barrier = pltpu.get_barrier_semaphore()
    mates = [{"expert": core_mate}, {"expert": chip_mate}]
    mates += [{"section": following}, {"section": previous}]
    others = [(group + d) % experts for d in range(1, experts)]
    mates += [{"expert": other * replicas + replica} for other in others]
    for mate in mates:
        pl.semaphore_signal(barrier, inc=1, device_id=mate, device_id_type=MESH)
    pl.semaphore_wait(barrier, len(mates))

    weights = [w_down, w_gate, w_up]
    started = []

    def quarter_copy(which, place, mate, source):
        copy = pltpu.make_async_remote_copy(
            src_ref=source,
            dst_ref=weights[which].at[pl.ds(place * quarter, quarter)],
            send_sem=quarter_send.at[place, which],
            recv_sem=quarter_recv.at[place, which],
            device_id={"expert": mate},
            device_id_type=MESH,
        )
        copy.start()
        started.append(copy)
        return copy

    def row_block(ref, index):
        return ref.at[pl.ds(pl.multiple_of(index * capacity, capacity), capacity)]

    def trade(source, target, send_sem, recv_sem):
        copies = []
        for place, other in enumerate(others):
            copy = pltpu.make_async_remote_copy(
                src_ref=row_block(source, other),
                dst_ref=row_block(target, group),
                send_sem=send_sem.at[place],
                recv_sem=recv_sem.at[place],
                device_id={"expert": other * replicas + replica},
                device_id_type=MESH,
            )
            copy.start()
            copies.append(copy)
        started.extend(copies)
        own = pl.ds(pl.multiple_of(group * capacity, capacity), capacity)
        target[own, :] = source[own, :]
        return copies

    across = []
    for which, source in enumerate((down_ref, gate_ref, up_ref)):
        across.append(quarter_copy(which, 2, chip_mate, source))
        quarter_copy(which, 1, core_mate, source)

    gain = gain_ref[...]
    router = router_ref[...]
    fwd_inverse, fwd_normed = normalize(fwd_in[...], gain)
    del fwd_inverse
    fwd_route = routing(fwd_normed, router, ids_ref[0], keep_ref[0], capacity)
    sent[0] = matmul(fwd_route[5], fwd_normed).astype(BF16)
    moves = [trade(sent.at[0], got.at[0], row_send.at[0], row_recv.at[0])]

    bwd_inverse, bwd_normed = normalize(bwd_in[...], gain)
    bwd_route = routing(bwd_normed, router, ids_ref[1], keep_ref[1], capacity)
    sent[1] = matmul(bwd_route[5], bwd_normed).astype(BF16)
    moves.append(trade(sent.at[1], got.at[1], row_send.at[1], row_recv.at[1]))
    sent[2] = matmul(bwd_route[5], grad_in[...]).astype(BF16)
    moves.append(trade(sent.at[2], got.at[2], row_send.at[2], row_recv.at[2]))

    for target, source in zip(weights, (down_ref, gate_ref, up_ref)):
        target[0:quarter, :] = source[...]
    for which, copy in enumerate(across):
        copy.wait_recv()
        quarter_copy(which, 3, core_mate, weights[which].at[pl.ds(2 * quarter, quarter)])
    for place in (1, 3):
        for which in range(3):
            pltpu.make_async_remote_copy(
                src_ref=down_ref,
                dst_ref=weights[which].at[pl.ds(place * quarter, quarter)],
                send_sem=quarter_send.at[place, which],
                recv_sem=quarter_recv.at[place, which],
                device_id={"expert": core_mate},
                device_id_type=MESH,
            ).wait_recv()

    step = 256 if hidden % 256 == 0 else quarter
    wide = 512 if width % 512 == 0 else width

    def part(index, size):
        return pl.ds(pl.multiple_of(index * size, size), size)

    for copy in moves[0]:
        copy.wait_recv()

    @pl.loop(0, hidden // step)
    def _(h):
        rows = got[0]
        pre_gate = rows_by_rows(rows, w_gate[part(h, step), :])
        pre_up = rows_by_rows(rows, w_up[part(h, step), :])
        inner[:, part(h, step)] = (pre_gate * jax.nn.sigmoid(pre_gate) * pre_up).astype(BF16)

    @pl.loop(0, width // wide)
    def _(c):
        done[0, :, part(c, wide)] = matmul(inner[...], w_down[:, part(c, wide)]).astype(BF16)

    returns = [trade(done.at[0], back.at[0], back_send.at[0], back_recv.at[0])]

    for copy in moves[1] + moves[2]:
        copy.wait_recv()

    def backward_step(h, change):
        rows = got[1]
        pre_gate = rows_by_rows(rows, w_gate[part(h, step), :])
        pre_up = rows_by_rows(rows, w_up[part(h, step), :])
        pulled = rows_by_rows(got[2], w_down[part(h, step), :])
        sigma = jax.nn.sigmoid(pre_gate)
        act = (pre_gate * sigma * pre_up).astype(BF16).astype(F32)
        grad_gate[:, part(h, step)] = (
            pulled * pre_up * sigma * (1.0 + pre_gate * (1.0 - sigma))
        ).astype(BF16)
        grad_up[:, part(h, step)] = (pulled * pre_gate * sigma).astype(BF16)
        return change + jnp.sum(act * pulled, axis=1, keepdims=True)

    change = lax.fori_loop(0, hidden // step, backward_step, jnp.zeros((slots, 1), F32))
    change_done[...] = jnp.broadcast_to(change, change_done.shape).astype(BF16)
    change_moves = trade(change_done, change_back, back_send.at[2], back_recv.at[2])

    @pl.loop(0, width // wide)
    def _(c):
        total = matmul(grad_gate[...], w_gate[:, part(c, wide)])
        total += matmul(grad_up[...], w_up[:, part(c, wide)])
        done[1, :, part(c, wide)] = total.astype(BF16)

    returns.append(trade(done.at[1], back.at[1], back_send.at[1], back_recv.at[1]))

    for copy in returns[0]:
        copy.wait_recv()
    fwd_pick = pickers(fwd_route[4], slots)
    fwd_scale = fwd_route[3]

    @pl.loop(0, width // wide)
    def _(c):
        total = fwd_in[:, part(c, wide)].astype(F32)
        mixed = None
        for pick, scale in zip(fwd_pick, fwd_scale):
            term = scale * matmul(pick, back[0, :, part(c, wide)])
            mixed = term if mixed is None else mixed + term
        staged[0, :, part(c, wide)] = (total + mixed).astype(BF16)

    hand_fwd = pltpu.make_async_remote_copy(
        src_ref=staged.at[0],
        dst_ref=fwd_out.at[0],
        send_sem=hand_send.at[0],
        recv_sem=hand_recv.at[0],
        device_id={"section": following},
        device_id_type=MESH,
    )
    hand_fwd.start()

    for copy in change_moves + returns[1]:
        copy.wait_recv()
    chosen, probs, kept, scale, slot, _ = bwd_route
    pick = pickers(slot, slots)
    moved = [kept[k] * matmul(pick[k], change_back[...])[:, 0:1] for k in range(len(pick))]
    balance = functools.reduce(jnp.add, [probs[k] * moved[k] for k in range(len(pick))])
    logit_grad = [probs[k] * (moved[k] - balance) for k in range(len(pick))]
    dense = functools.reduce(
        jnp.add, [jnp.where(chosen[k], logit_grad[k], 0.0) for k in range(len(pick))]
    )
    dense_high = dense.astype(BF16)
    dense_low = (dense - dense_high.astype(F32)).astype(BF16)

    span = 32 if tokens % 32 == 0 else tokens
    hand_bwd = []
    for piece in range(tokens // span):
        own = slice(piece * span, (piece + 1) * span)

        def gather_step(c, dots):
            total = None
            for k in range(len(pick)):
                term = scale[k][own] * matmul(pick[k][own], back[1, :, part(c, wide)])
                total = term if total is None else total + term
            near_router = router_ref[:, part(c, wide)]
            total += matmul(dense_high[own], near_router) + matmul(dense_low[own], near_router)
            gained = total * gain_ref[:, part(c, wide)]
            weighted[own, part(c, wide)] = gained
            plain = bwd_in[own, part(c, wide)].astype(F32)
            return dots + jnp.sum(gained * plain, axis=1, keepdims=True)

        dots = lax.fori_loop(0, width // wide, gather_step, jnp.zeros((span, 1), F32))
        inverse = bwd_inverse[own]
        factor = inverse * inverse * (dots * (1.0 / width))
        norm_grad = inverse * (weighted[own, :] - bwd_in[own, :].astype(F32) * factor)
        staged[1, own, :] = (grad_in[own, :].astype(F32) + norm_grad).astype(BF16)
        copy = pltpu.make_async_remote_copy(
            src_ref=staged.at[1, pl.ds(piece * span, span)],
            dst_ref=bwd_out.at[0, pl.ds(piece * span, span)],
            send_sem=hand_send.at[1 + piece],
            recv_sem=hand_recv.at[1 + piece],
            device_id={"section": previous},
            device_id_type=MESH,
        )
        copy.start()
        hand_bwd.append(copy)
    for copy in started:
        copy.wait_send()
    hand_fwd.wait()
    for copy in hand_bwd:
        copy.wait()


def on_device(
    section_input,
    saved_input,
    grad_input,
    expert_ids,
    keep_mask,
    norm_gain,
    router_weight,
    gate_weight,
    up_weight,
    down_weight,
):
    tokens, width = section_input.shape[1:]
    experts = router_weight.shape[2]
    top = expert_ids.shape[3]
    replicas = lax.axis_size("expert") // experts
    sections = lax.axis_size("section")
    capacity = 4 * tokens * top // (3 * experts)
    slots = experts * capacity
    quarter = down_weight.shape[1]
    hidden = quarter * replicas
    dma = pltpu.SemaphoreType.DMA
    vmem = pl.BlockSpec(memory_space=pltpu.VMEM)
    result = jax.ShapeDtypeStruct((1, tokens, width), BF16)
    return pl.pallas_call(
        functools.partial(layer, experts, replicas, sections, capacity),
        out_shape=(result, result),
        in_specs=[vmem] * 10,
        out_specs=(pl.BlockSpec(memory_space=pl.ANY),) * 2,
        scratch_shapes=[
            pltpu.VMEM((hidden, width), BF16),
            pltpu.VMEM((hidden, width), BF16),
            pltpu.VMEM((hidden, width), BF16),
            pltpu.VMEM((3, slots, width), BF16),
            pltpu.VMEM((3, slots, width), BF16),
            pltpu.VMEM((2, slots, width), BF16),
            pltpu.VMEM((2, slots, width), BF16),
            pltpu.VMEM((slots, 128), BF16),
            pltpu.VMEM((slots, 128), BF16),
            pltpu.VMEM((slots, hidden), BF16),
            pltpu.VMEM((slots, hidden), BF16),
            pltpu.VMEM((slots, hidden), BF16),
            pltpu.VMEM((tokens, width), F32),
            pltpu.VMEM((2, tokens, width), BF16),
            dma((4, 3)),
            dma((4, 3)),
            dma((3, experts - 1)),
            dma((3, experts - 1)),
            dma((3, experts - 1)),
            dma((3, experts - 1)),
            dma((1 + tokens // 32,)),
            dma((1 + tokens // 32,)),
        ],
        compiler_params=pltpu.CompilerParams(
            collective_id=0, has_side_effects=True, vmem_limit_bytes=56 * 1024 * 1024
        ),
    )(
        section_input[0],
        saved_input[0],
        grad_input[0],
        jnp.swapaxes(expert_ids[0], 1, 2),
        jnp.swapaxes(keep_mask[0], 1, 2),
        norm_gain,
        router_weight[0].T,
        gate_weight[0].T,
        up_weight[0].T,
        down_weight[0],
    )


def solution(mesh):
    return jax.shard_map(
        on_device,
        mesh=mesh,
        in_specs=(
            P("section", "expert", None),
            P("section", "expert", None),
            P("section", "expert", None),
            P("section", None, "expert", None),
            P("section", None, "expert", None),
            P("section", None),
            P("section", None, None),
            P("section", None, "expert"),
            P("section", None, "expert"),
            P("section", "expert", None),
        ),
        out_specs=(P("section", "expert", None), P("section", "expert", None)),
        check_vma=False,
    )
```

```python
import functools

import jax
import jax.numpy as jnp
from jax import lax
from jax.experimental import pallas as pl
from jax.experimental.pallas import tpu as pltpu
from jax.sharding import PartitionSpec as P

EPS = 1e-06
KEEP_SCALE = 8.0 / 7.0
MESH = pl.DeviceIdType.MESH
F32 = jnp.float32
BF16 = jnp.bfloat16


def rows_by_rows(left, right):
    return lax.dot_general(left, right, (((1,), (1,)), ((), ())), preferred_element_type=F32)


def matmul(left, right):
    return jnp.dot(left, right, preferred_element_type=F32)


def normalize(hidden, gain):
    plain = hidden.astype(F32)
    inverse = lax.rsqrt(jnp.mean(plain * plain, axis=-1, keepdims=True) + EPS)
    return inverse, (plain * inverse * gain).astype(BF16)


def routing(normed, router, id_rows, keep_rows, capacity):
    tokens, experts = normed.shape[0], router.shape[0]
    top = id_rows.shape[0]
    logits = rows_by_rows(normed, router)
    lane = lax.broadcasted_iota(jnp.int32, (tokens, experts), 1)
    row = lax.broadcasted_iota(jnp.int32, (tokens, tokens), 0)
    column = lax.broadcasted_iota(jnp.int32, (tokens, tokens), 1)

    def upright(line):
        spread_out = jnp.where(row == column, line.astype(F32), 0.0)
        return jnp.sum(spread_out, axis=1, keepdims=True)

    ids = [upright(id_rows[k : k + 1, :]) for k in range(top)]
    chosen = [i == lane.astype(F32) for i in ids]
    picked = [jnp.sum(jnp.where(c, logits, 0.0), axis=1, keepdims=True) for c in chosen]
    probs = []
    for k in range(top):
        spread = functools.reduce(jnp.add, [jnp.exp(p - picked[k]) for p in picked])
        probs.append(1.0 / spread)
    kept = [upright(keep_rows[k : k + 1, :]) * KEEP_SCALE for k in range(top)]
    scale = [kept[k] * probs[k] for k in range(top)]
    named = functools.reduce(jnp.add, [jnp.where(c, 1.0, 0.0) for c in chosen])
    earlier = jnp.where(column < row, 1.0, 0.0).astype(BF16)
    rank = matmul(earlier, named.astype(BF16))
    place = lane.astype(F32) * capacity + rank
    slot = [jnp.sum(jnp.where(c, place, 0.0), axis=1, keepdims=True) for c in chosen]
    along = [jnp.sum(jnp.where(row == column, s, 0.0), axis=0, keepdims=True) for s in slot]
    table = lax.broadcasted_iota(jnp.int32, (experts * capacity, tokens), 0).astype(F32)
    fill = functools.reduce(jnp.add, [jnp.where(table == a, 1.0, 0.0) for a in along]).astype(BF16)
    return chosen, probs, kept, scale, slot, fill


def pickers(slot, slots):
    tokens = slot[0].shape[0]
    lane = lax.broadcasted_iota(jnp.int32, (tokens, slots), 1).astype(F32)
    return [jnp.where(lane == s, 1.0, 0.0).astype(BF16) for s in slot]


def layer(
    experts,
    replicas,
    sections,
    capacity,
    fwd_in,
    bwd_in,
    grad_in,
    ids_ref,
    keep_ref,
    gain_ref,
    router_ref,
    gate_ref,
    up_ref,
    down_ref,
    fwd_out,
    bwd_out,
    w_gate,
    w_up,
    w_down,
    sent,
    got,
    done,
    back,
    change_done,
    change_back,
    inner,
    grad_gate,
    grad_up,
    weighted,
    staged,
    quarter_send,
    quarter_recv,
    row_send,
    row_recv,
    back_send,
    back_recv,
    hand_send,
    hand_recv,
):
    section = lax.axis_index("section")
    me = lax.axis_index("expert")
    group, replica = me // replicas, me % replicas
    tokens, width = fwd_in.shape
    quarter = down_ref.shape[0]
    hidden = quarter * replicas
    slots = experts * capacity
    core_mate = group * replicas + (replica + 1 - 2 * (replica % 2))
    chip_mate = group * replicas + (replica + 2) % replicas
    following = (section + 1) % sections
    previous = (section + sections - 1) % sections

    barrier = pltpu.get_barrier_semaphore()
    mates = [{"expert": core_mate}, {"expert": chip_mate}]
    mates += [{"section": following}, {"section": previous}]
    others = [(group + d) % experts for d in range(1, experts)]
    mates += [{"expert": other * replicas + replica} for other in others]
    for mate in mates:
        pl.semaphore_signal(barrier, inc=1, device_id=mate, device_id_type=MESH)
    pl.semaphore_wait(barrier, len(mates))

    weights = [w_down, w_gate, w_up]
    started = []

    def quarter_copy(which, place, mate, source):
        copy = pltpu.make_async_remote_copy(
            src_ref=source,
            dst_ref=weights[which].at[pl.ds(place * quarter, quarter)],
            send_sem=quarter_send.at[place, which],
            recv_sem=quarter_recv.at[place, which],
            device_id={"expert": mate},
            device_id_type=MESH,
        )
        copy.start()
        started.append(copy)
        return copy

    def row_block(ref, index):
        return ref.at[pl.ds(pl.multiple_of(index * capacity, capacity), capacity)]

    def trade(source, target, send_sem, recv_sem):
        copies = []
        for place, other in enumerate(others):
            copy = pltpu.make_async_remote_copy(
                src_ref=row_block(source, other),
                dst_ref=row_block(target, group),
                send_sem=send_sem.at[place],
                recv_sem=recv_sem.at[place],
                device_id={"expert": other * replicas + replica},
                device_id_type=MESH,
            )
            copy.start()
            copies.append(copy)
        started.extend(copies)
        own = pl.ds(pl.multiple_of(group * capacity, capacity), capacity)
        target[own, :] = source[own, :]
        return copies

    across = []
    for which, source in enumerate((down_ref, gate_ref, up_ref)):
        across.append(quarter_copy(which, 2, chip_mate, source))
        quarter_copy(which, 1, core_mate, source)

    gain = gain_ref[...]
    router = router_ref[...]
    fwd_inverse, fwd_normed = normalize(fwd_in[...], gain)
    del fwd_inverse
    fwd_route = routing(fwd_normed, router, ids_ref[0], keep_ref[0], capacity)
    sent[0] = matmul(fwd_route[5], fwd_normed).astype(BF16)
    moves = [trade(sent.at[0], got.at[0], row_send.at[0], row_recv.at[0])]

    bwd_inverse, bwd_normed = normalize(bwd_in[...], gain)
    bwd_route = routing(bwd_normed, router, ids_ref[1], keep_ref[1], capacity)
    sent[1] = matmul(bwd_route[5], bwd_normed).astype(BF16)
    moves.append(trade(sent.at[1], got.at[1], row_send.at[1], row_recv.at[1]))
    sent[2] = matmul(bwd_route[5], grad_in[...]).astype(BF16)
    moves.append(trade(sent.at[2], got.at[2], row_send.at[2], row_recv.at[2]))

    for target, source in zip(weights, (down_ref, gate_ref, up_ref)):
        target[0:quarter, :] = source[...]
    for which, copy in enumerate(across):
        copy.wait_recv()
        quarter_copy(which, 3, core_mate, weights[which].at[pl.ds(2 * quarter, quarter)])
    for place in (1, 3):
        for which in range(3):
            pltpu.make_async_remote_copy(
                src_ref=down_ref,
                dst_ref=weights[which].at[pl.ds(place * quarter, quarter)],
                send_sem=quarter_send.at[place, which],
                recv_sem=quarter_recv.at[place, which],
                device_id={"expert": core_mate},
                device_id_type=MESH,
            ).wait_recv()

    step = 256 if hidden % 256 == 0 else quarter
    wide = 512 if width % 512 == 0 else width

    def part(index, size):
        return pl.ds(pl.multiple_of(index * size, size), size)

    for copy in moves[0]:
        copy.wait_recv()

    @pl.loop(0, hidden // step)
    def _(h):
        rows = got[0]
        pre_gate = rows_by_rows(rows, w_gate[part(h, step), :])
        pre_up = rows_by_rows(rows, w_up[part(h, step), :])
        inner[:, part(h, step)] = (pre_gate * jax.nn.sigmoid(pre_gate) * pre_up).astype(BF16)

    @pl.loop(0, width // wide)
    def _(c):
        done[0, :, part(c, wide)] = matmul(inner[...], w_down[:, part(c, wide)]).astype(BF16)

    returns = [trade(done.at[0], back.at[0], back_send.at[0], back_recv.at[0])]

    for copy in moves[1] + moves[2]:
        copy.wait_recv()

    def backward_step(h, change):
        rows = got[1]
        pre_gate = rows_by_rows(rows, w_gate[part(h, step), :])
        pre_up = rows_by_rows(rows, w_up[part(h, step), :])
        pulled = rows_by_rows(got[2], w_down[part(h, step), :])
        sigma = jax.nn.sigmoid(pre_gate)
        act = (pre_gate * sigma * pre_up).astype(BF16).astype(F32)
        grad_gate[:, part(h, step)] = (
            pulled * pre_up * sigma * (1.0 + pre_gate * (1.0 - sigma))
        ).astype(BF16)
        grad_up[:, part(h, step)] = (pulled * pre_gate * sigma).astype(BF16)
        return change + jnp.sum(act * pulled, axis=1, keepdims=True)

    change = lax.fori_loop(0, hidden // step, backward_step, jnp.zeros((slots, 1), F32))
    change_done[...] = jnp.broadcast_to(change, change_done.shape).astype(BF16)
    change_moves = trade(change_done, change_back, back_send.at[2], back_recv.at[2])

    half = width // 2
    sides = []
    for side in range(2):

        @pl.loop(side * (half // wide), (side + 1) * (half // wide))
        def _(c):
            total = matmul(grad_gate[...], w_gate[:, part(c, wide)])
            total += matmul(grad_up[...], w_up[:, part(c, wide)])
            done[1, :, part(c, wide)] = total.astype(BF16)

        columns = pl.ds(side * half, half)
        sides += trade(
            done.at[1, :, columns],
            back.at[1, :, columns],
            back_send.at[1 + 2 * side],
            back_recv.at[1 + 2 * side],
        )
    returns.append(sides)

    for copy in returns[0]:
        copy.wait_recv()
    fwd_pick = pickers(fwd_route[4], slots)
    fwd_scale = fwd_route[3]

    @pl.loop(0, width // wide)
    def _(c):
        total = fwd_in[:, part(c, wide)].astype(F32)
        mixed = None
        for pick, scale in zip(fwd_pick, fwd_scale):
            term = scale * matmul(pick, back[0, :, part(c, wide)])
            mixed = term if mixed is None else mixed + term
        staged[0, :, part(c, wide)] = (total + mixed).astype(BF16)

    hand_fwd = pltpu.make_async_remote_copy(
        src_ref=staged.at[0],
        dst_ref=fwd_out.at[0],
        send_sem=hand_send.at[0],
        recv_sem=hand_recv.at[0],
        device_id={"section": following},
        device_id_type=MESH,
    )
    hand_fwd.start()

    for copy in change_moves + returns[1]:
        copy.wait_recv()
    chosen, probs, kept, scale, slot, _ = bwd_route
    pick = pickers(slot, slots)
    moved = [kept[k] * matmul(pick[k], change_back[...])[:, 0:1] for k in range(len(pick))]
    balance = functools.reduce(jnp.add, [probs[k] * moved[k] for k in range(len(pick))])
    logit_grad = [probs[k] * (moved[k] - balance) for k in range(len(pick))]
    dense = functools.reduce(
        jnp.add, [jnp.where(chosen[k], logit_grad[k], 0.0) for k in range(len(pick))]
    )
    dense_high = dense.astype(BF16)
    dense_low = (dense - dense_high.astype(F32)).astype(BF16)

    span = 32 if tokens % 32 == 0 else tokens
    hand_bwd = []
    for piece in range(tokens // span):
        own = slice(piece * span, (piece + 1) * span)

        def gather_step(c, dots):
            total = None
            for k in range(len(pick)):
                term = scale[k][own] * matmul(pick[k][own], back[1, :, part(c, wide)])
                total = term if total is None else total + term
            near_router = router_ref[:, part(c, wide)]
            total += matmul(dense_high[own], near_router) + matmul(dense_low[own], near_router)
            gained = total * gain_ref[:, part(c, wide)]
            weighted[own, part(c, wide)] = gained
            plain = bwd_in[own, part(c, wide)].astype(F32)
            return dots + jnp.sum(gained * plain, axis=1, keepdims=True)

        dots = lax.fori_loop(0, width // wide, gather_step, jnp.zeros((span, 1), F32))
        inverse = bwd_inverse[own]
        factor = inverse * inverse * (dots * (1.0 / width))
        norm_grad = inverse * (weighted[own, :] - bwd_in[own, :].astype(F32) * factor)
        staged[1, own, :] = (grad_in[own, :].astype(F32) + norm_grad).astype(BF16)
        copy = pltpu.make_async_remote_copy(
            src_ref=staged.at[1, pl.ds(piece * span, span)],
            dst_ref=bwd_out.at[0, pl.ds(piece * span, span)],
            send_sem=hand_send.at[1 + piece],
            recv_sem=hand_recv.at[1 + piece],
            device_id={"section": previous},
            device_id_type=MESH,
        )
        copy.start()
        hand_bwd.append(copy)
    for copy in started:
        copy.wait_send()
    hand_fwd.wait()
    for copy in hand_bwd:
        copy.wait()


def on_device(
    section_input,
    saved_input,
    grad_input,
    expert_ids,
    keep_mask,
    norm_gain,
    router_weight,
    gate_weight,
    up_weight,
    down_weight,
):
    tokens, width = section_input.shape[1:]
    experts = router_weight.shape[2]
    top = expert_ids.shape[3]
    replicas = lax.axis_size("expert") // experts
    sections = lax.axis_size("section")
    capacity = 4 * tokens * top // (3 * experts)
    slots = experts * capacity
    quarter = down_weight.shape[1]
    hidden = quarter * replicas
    dma = pltpu.SemaphoreType.DMA
    vmem = pl.BlockSpec(memory_space=pltpu.VMEM)
    result = jax.ShapeDtypeStruct((1, tokens, width), BF16)
    return pl.pallas_call(
        functools.partial(layer, experts, replicas, sections, capacity),
        out_shape=(result, result),
        in_specs=[vmem] * 10,
        out_specs=(pl.BlockSpec(memory_space=pl.ANY),) * 2,
        scratch_shapes=[
            pltpu.VMEM((hidden, width), BF16),
            pltpu.VMEM((hidden, width), BF16),
            pltpu.VMEM((hidden, width), BF16),
            pltpu.VMEM((3, slots, width), BF16),
            pltpu.VMEM((3, slots, width), BF16),
            pltpu.VMEM((2, slots, width), BF16),
            pltpu.VMEM((2, slots, width), BF16),
            pltpu.VMEM((slots, 128), BF16),
            pltpu.VMEM((slots, 128), BF16),
            pltpu.VMEM((slots, hidden), BF16),
            pltpu.VMEM((slots, hidden), BF16),
            pltpu.VMEM((slots, hidden), BF16),
            pltpu.VMEM((tokens, width), F32),
            pltpu.VMEM((2, tokens, width), BF16),
            dma((4, 3)),
            dma((4, 3)),
            dma((3, experts - 1)),
            dma((3, experts - 1)),
            dma((4, experts - 1)),
            dma((4, experts - 1)),
            dma((1 + tokens // 32,)),
            dma((1 + tokens // 32,)),
        ],
        compiler_params=pltpu.CompilerParams(
            collective_id=0, has_side_effects=True, vmem_limit_bytes=56 * 1024 * 1024
        ),
    )(
        section_input[0],
        saved_input[0],
        grad_input[0],
        jnp.swapaxes(expert_ids[0], 1, 2),
        jnp.swapaxes(keep_mask[0], 1, 2),
        norm_gain,
        router_weight[0].T,
        gate_weight[0].T,
        up_weight[0].T,
        down_weight[0],
    )


def solution(mesh):
    return jax.shard_map(
        on_device,
        mesh=mesh,
        in_specs=(
            P("section", "expert", None),
            P("section", "expert", None),
            P("section", "expert", None),
            P("section", None, "expert", None),
            P("section", None, "expert", None),
            P("section", None),
            P("section", None, None),
            P("section", None, "expert"),
            P("section", None, "expert"),
            P("section", "expert", None),
        ),
        out_specs=(P("section", "expert", None), P("section", "expert", None)),
        check_vma=False,
    )
```
